512 devices in a mesh: replica: 16 (over y_lo, x, core), fsdp: 32 (over z, y_hi).
Axes of the slice: x: 4, y: 4 (y_hi: 2, y_lo: 2; y = y_hi * 2 + y_lo), z: 16, core: 2. Of those that a mesh axis runs over, the one named last changes fastest.
Arguments:
- tokens: bfloat16 [65536, 4096], P(('replica', 'fsdp')), may hold values from -6 to 6
- v_weight: bfloat16 [16, 4096, 512], P('replica', 'fsdp'), may hold values from -0.09375 to 0.09375
- out_grad: bfloat16 [65536, 512], P(('replica', 'fsdp')), may hold values from -6 to 6
- outer_params: float32 [4, 4096, 512], P(None, 'fsdp'), may hold values from -6 to 6
- momentum: float32 [4, 4096, 512], P(None, 'fsdp'), may hold values from -4 to 4
- snapshot: bfloat16 [16, 4, 4096, 512], P('replica', None, 'fsdp'), may hold values from -6 to 6
- frag_index: int32 [1], replicated, may hold values from 0 to 3
Outputs:
- values: bfloat16 [65536, 512], P(('replica', 'fsdp'))
- input_grad: bfloat16 [65536, 4096], P(('replica', 'fsdp'))
- weight_grad: bfloat16 [16, 4096, 512], P('replica', 'fsdp')
- new_outer: float32 [4, 4096, 512], P(None, 'fsdp')
- new_momentum: float32 [4, 4096, 512], P(None, 'fsdp')
The draws below stay inside these ranges and needn't reach their ends.
All inputs are finite; a program needn't handle non-finite values.
Results may differ from the reference program's by a relative error of at most 0.001.
Values may be sent and summed in bfloat16 or wider, within the bound.
No kernel may reach another device: no remote copies, remote signals or barrier semaphores. Data moves between devices by JAX's collectives and lax.ppermute only.
A program may use at most 64 MiB of HBM per device.

```python
import math
import jax
import jax.numpy as jnp
from jax import lax

D = 4096
KVW = 512
FRAGS = 4
REP_TOKENS = 4096
TOKENS = 65536
N_REPLICA = 16


def block_levels(own_key, extent, shards, smallest, top_value):
    loudness = 1.0
    for axis_at, shards_of in shards:
        steps = jax.random.uniform(jax.random.fold_in(jax.random.fold_in(own_key, 6), axis_at), (shards_of,), jnp.float32, smallest / len(shards), top_value / len(shards))
        loudness = loudness * jnp.repeat(jnp.exp(steps), extent[axis_at] // shards_of).reshape((-1,) + (1,) * (len(extent) - 1 - axis_at))
    return loudness


def bell_draw(own_key, shape, scale, bound, split=(), dtype=jnp.bfloat16):
    loudness = block_levels(own_key, shape, split, -0.22, 0.18) if split else 1.0
    entries = jax.random.normal(own_key, shape, jnp.float32) * scale * loudness
    return jnp.minimum(jnp.maximum(entries, -bound), bound).astype(dtype)


def setup_inputs(seed: int = 0) -> dict:
    key_list = jax.random.split(jax.random.key(seed), 8)
    return {
        "tokens": bell_draw(key_list[0], (TOKENS, D), 1.0, 6.0, ((0, 512),)),
        "v_weight": bell_draw(key_list[1], (N_REPLICA, D, KVW), D ** -0.5, 0.09375, ((0, 16), (1, 32))),
        "out_grad": bell_draw(key_list[2], (TOKENS, KVW), 1.0, 6.0, ((0, 512),)),
        "outer_params": bell_draw(key_list[3], (FRAGS, D, KVW), 1.0, 6.0, ((1, 32),), jnp.float32),
        "momentum": bell_draw(key_list[4], (FRAGS, D, KVW), 0.5, 4.0, ((1, 32),), jnp.float32),
        "snapshot": bell_draw(key_list[5], (N_REPLICA, FRAGS, D, KVW), 1.0, 6.0, ((0, 16), (2, 32))),
        "frag_index": jax.random.randint(key_list[6], (1,), 0, FRAGS).astype(jnp.int32),
    }


def per_replica(packed):
    rows, weight, grads = packed
    values = jnp.dot(rows, weight, preferred_element_type=jnp.float32).astype(jnp.bfloat16)
    input_grad = jnp.dot(grads, weight.T, preferred_element_type=jnp.float32).astype(jnp.bfloat16)
    summed = jnp.dot(rows.T, grads, preferred_element_type=jnp.float32)
    weight_grad = (summed * (1.0 / math.sqrt(REP_TOKENS))).astype(jnp.bfloat16)
    return (values, input_grad, weight_grad)

def reference(tokens, v_weight, out_grad, outer_params, momentum, snapshot, frag_index):
    rows = tokens.reshape(N_REPLICA, REP_TOKENS, D)
    grads = out_grad.reshape(N_REPLICA, REP_TOKENS, KVW)
    values, input_grad, weight_grad = lax.map(per_replica, (rows, v_weight, grads))
    chosen = frag_index[0]
    outer_now = lax.dynamic_index_in_dim(outer_params, chosen, 0, keepdims=False)
    moment_now = lax.dynamic_index_in_dim(momentum, chosen, 0, keepdims=False)
    snaps = lax.dynamic_index_in_dim(snapshot, chosen, 1, keepdims=False).astype(jnp.float32)
    pseudo_grad = lax.optimization_barrier(jnp.sum(outer_now[None] - snaps, axis=0)) / N_REPLICA
    moment_new = 0.9 * moment_now + pseudo_grad
    outer_new = outer_now - 0.7 * (pseudo_grad + 0.9 * moment_new)
    new_momentum = lax.dynamic_update_index_in_dim(momentum, moment_new, chosen, 0)
    new_outer = lax.dynamic_update_index_in_dim(outer_params, outer_new, chosen, 0)
    return (values.reshape(TOKENS, KVW), input_grad.reshape(TOKENS, D), weight_grad, new_outer, new_momentum)
```

```python
import functools
import math

import jax
import jax.numpy as jnp
from jax import lax
from jax.experimental import pallas as pl
from jax.experimental.pallas import tpu as pltpu
from jax.sharding import Mesh
from jax.sharding import PartitionSpec as P

REPLICA = ("ylo", "x", "core")
EVERY = REPLICA + ("z", "yhi")
F32, BF16 = jnp.float32, jnp.bfloat16
VMEM = pl.BlockSpec(memory_space=pltpu.VMEM)
SMEM = pl.BlockSpec(memory_space=pltpu.SMEM)


def local(kernel, outs, name, ins):
    return pl.pallas_call(
        kernel,
        out_shape=[jax.ShapeDtypeStruct(s, d) for s, d in outs],
        in_specs=[SMEM] + [VMEM] * (len(ins) - 1),
        out_specs=[VMEM] * len(outs),
        name=name,
        compiler_params=pltpu.CompilerParams(vmem_limit_bytes=40 * 2**20),
    )(*ins)


def lanes(block, width=128):
    return pl.ds(pl.multiple_of(block * width, width), width)


def pack_kernel(place, tokens, out_grad, *packs):
    for p, pack in enumerate(packs):
        wanted = jnp.bitwise_xor(place[0], p)
        for m in range(8):
            pack[:, m * 128 : (m + 1) * 128] = tokens[:, lanes(4 * m + wanted)]
        pack[:, 1024:] = out_grad[...]


def weight_grad_kernel(place, p0, p1, p2, p3, out):
    both = jnp.concatenate([p[...] for p in (p0, p1, p2, p3)], axis=0)
    grads = both[:, 1024:]
    for half in range(4):
        cols = slice(half * 256, (half + 1) * 256)
        out[cols, :] = lax.dot_general(
            both[:, cols], grads, (((0,), (0,)), ((), ())), preferred_element_type=F32
        )


def project_kernel(place, p0, p1, p2, p3, own, f1, f2, f3, b1, b2, b3, far_lo, far_hi, *rest):
    values, grads, weight = rest[:4], rest[4:8], rest[8]
    m = place[1]

    def rows(shift, extra=0, size=128):
        return pl.ds(pl.multiple_of(lax.rem(m + 8 + shift, 8) * 128 + extra, 64), size)

    for shift, block in ((0, own), (-1, f1), (-2, f2), (-3, f3), (1, b1), (2, b2), (3, b3)):
        weight[rows(shift), :] = block[...]
    weight[rows(4, 0, 64), :] = far_lo[...]
    weight[rows(4, 64, 64), :] = far_hi[...]
    both = jnp.concatenate([p[...] for p in (p0, p1, p2, p3)], axis=0)
    total = jnp.dot(both[:, :1024], weight[...], preferred_element_type=F32)
    for p in range(4):
        values[p][...] = total[p * 128 : (p + 1) * 128]
    for part in range(4):
        cols = slice(part * 256, (part + 1) * 256)
        piece = lax.dot_general(
            both[:, 1024:], weight[cols, :], (((1,), (1,)), ((), ())), preferred_element_type=F32
        ).astype(BF16)
        for p in range(4):
            grads[p][:, cols] = piece[p * 128 : (p + 1) * 128]


def finish_kernel(place, v0, v1, v2, v3, g0, g1, g2, g3, values, input_grad):
    values[...] = (v0[...] + v1[...] + v2[...] + v3[...]).astype(BF16)
    for p, grad in enumerate((g0, g1, g2, g3)):
        wanted = jnp.bitwise_xor(place[0], p)
        for m in range(8):
            input_grad[:, lanes(4 * m + wanted)] = grad[:, m * 128 : (m + 1) * 128]


def outer_kernel(chosen, outer, momentum, snaps, new_outer, new_momentum):
    k = chosen[0]
    new_outer[...] = outer[...]
    new_momentum[...] = momentum[...]
    now = outer[k]
    pseudo = jnp.zeros_like(now)
    for r in range(16):
        pseudo += now - snaps[r].astype(F32)
    pseudo = pseudo * (1.0 / 16)
    moment = 0.9 * momentum[k] + pseudo
    new_momentum[k] = moment
    new_outer[k] = now - 0.7 * (pseudo + 0.9 * moment)


def partner(core, z):
    return z ^ 1 if core == 0 else ((z + 1) % 16 if z % 2 else (z - 1) % 16)


def swaps():
    z_pairs, diagonal = [], []
    for core in range(2):
        for z in range(16):
            here, there = core * 16 + z, core * 16 + partner(core, z)
            z_pairs.append((here, there))
            diagonal += [(2 * here + y, 2 * there + 1 - y) for y in range(2)]
    return (
        lambda a: a,
        lambda a: lax.ppermute(a, "yhi", [(0, 1), (1, 0)]),
        lambda a: lax.ppermute(a, ("core", "z"), z_pairs),
        lambda a: lax.ppermute(a, ("core", "z", "yhi"), diagonal),
    )


def body(tokens, v_weight, out_grad, outer_params, momentum, snapshot, frag_index):
    z, y = lax.axis_index("z"), lax.axis_index("yhi")
    place = jnp.stack([2 * lax.rem(z, 2) + y, lax.div(z, 2)]).astype(jnp.int32)
    swap = swaps()

    snap = lax.dynamic_index_in_dim(snapshot[0], frag_index[0], 0, keepdims=False)
    snaps = lax.all_gather(snap, REPLICA, axis=0)

    packs = local(pack_kernel, [((128, 1536), BF16)] * 4, "pack", (place, tokens, out_grad))
    packs = [swap[p](packs[p]) for p in range(4)]

    (partial,) = local(weight_grad_kernel, [((1024, 512), F32)], "weight_grad", (place, *packs))
    rings = [[z_of for z_of in range(16) if z_of % 2 == odd] for odd in range(2)]
    summed = lax.psum_scatter(partial, "z", scatter_dimension=0, axis_index_groups=rings, tiled=True)
    weight_grad = (summed * (1.0 / math.sqrt(4096))).astype(BF16)[None]

    own = v_weight[0]
    ahead = functools.partial(lax.ppermute, axis_name="z", perm=[(i, (i + 2) % 16) for i in range(16)])
    behind = functools.partial(lax.ppermute, axis_name="z", perm=[(i, (i - 2) % 16) for i in range(16)])
    fwd, bwd = [own], [own]
    for _ in range(3):
        fwd.append(ahead(fwd[-1]))
        bwd.append(behind(bwd[-1]))
    far = [ahead(fwd[-1][:64]), behind(bwd[-1][64:])]
    parts = pl.pallas_call(
        project_kernel,
        out_shape=[jax.ShapeDtypeStruct((128, 512), F32)] * 4 + [jax.ShapeDtypeStruct((128, 1024), BF16)] * 4,
        in_specs=[SMEM] + [VMEM] * 13,
        out_specs=[VMEM] * 8,
        scratch_shapes=[pltpu.VMEM((1024, 512), BF16)],
        name="project",
        compiler_params=pltpu.CompilerParams(vmem_limit_bytes=40 * 2**20),
    )(place, *packs, own, *fwd[1:], *bwd[1:], *far)
    parts = [swap[i % 4](part) for i, part in enumerate(parts)]
    values, input_grad = local(
        finish_kernel, [((128, 512), BF16), ((128, 4096), BF16)], "finish", (place, *parts)
    )

    new_outer, new_momentum = local(
        outer_kernel,
        [((4, 128, 512), F32)] * 2,
        "outer",
        (frag_index, outer_params, momentum, snaps),
    )
    return (values, input_grad, weight_grad, new_outer, new_momentum)


def solution(mesh):
    fine = Mesh(mesh.devices.reshape(2, 4, 2, 16, 2), EVERY)
    fsdp = ("z", "yhi")
    in_specs = (
        P(EVERY, None),
        P(REPLICA, fsdp, None),
        P(EVERY, None),
        P(None, fsdp, None),
        P(None, fsdp, None),
        P(REPLICA, None, fsdp, None),
        P(),
    )
    out_specs = (
        P(EVERY, None),
        P(EVERY, None),
        P(REPLICA, fsdp, None),
        P(None, fsdp, None),
        P(None, fsdp, None),
    )
    return jax.shard_map(body, mesh=fine, in_specs=in_specs, out_specs=out_specs, check_vma=False)
```

```python
import functools
import math

import jax
import jax.numpy as jnp
from jax import lax
from jax.experimental import pallas as pl
from jax.experimental.pallas import tpu as pltpu
from jax.sharding import Mesh
from jax.sharding import PartitionSpec as P

REPLICA = ("ylo", "x", "core")
EVERY = REPLICA + ("z", "yhi")
F32, BF16 = jnp.float32, jnp.bfloat16
VMEM = pl.BlockSpec(memory_space=pltpu.VMEM)
SMEM = pl.BlockSpec(memory_space=pltpu.SMEM)


def local(kernel, outs, name, ins):
    return pl.pallas_call(
        kernel,
        out_shape=[jax.ShapeDtypeStruct(s, d) for s, d in outs],
        in_specs=[SMEM] + [VMEM] * (len(ins) - 1),
        out_specs=[VMEM] * len(outs),
        name=name,
        compiler_params=pltpu.CompilerParams(vmem_limit_bytes=40 * 2**20),
    )(*ins)


def lanes(block, width=128):
    return pl.ds(pl.multiple_of(block * width, width), width)


def pack_kernel(place, tokens, out_grad, *packs):
    for p, pack in enumerate(packs):
        wanted = jnp.bitwise_xor(place[0], min(p, 3))
        for m in range(8):
            pack[:, m * 128 : (m + 1) * 128] = tokens[:, lanes(4 * m + wanted)]
        if p < 4:
            pack[:, 1024:] = out_grad[...]


def weight_grad_kernel(place, p0, p1, p2, p3, out):
    both = jnp.concatenate([p[...] for p in (p0, p1, p2, p3)], axis=0)
    grads = both[:, 1024:]
    for part in range(4):
        cols = slice(part * 256, (part + 1) * 256)
        out[cols, :] = lax.dot_general(
            both[:, cols], grads, (((0,), (0,)), ((), ())), preferred_element_type=F32
        )


def project_kernel(place, own, own_more, other, other_more, gathered, v_own, v_other, g_own, g_other, weight):
    parity = lax.shift_right_logical(place[0], 1)
    for half in range(2):
        for m in range(8):
            row = pl.multiple_of((2 * m + jnp.bitwise_xor(parity, half)) * 128, 128)
            weight[half * 1024 + m * 128 : half * 1024 + (m + 1) * 128, :] = gathered[pl.ds(row, 128), :]
    rows = jnp.concatenate([own[:, :1024], other[:, :1024]], axis=0)
    rows_more = jnp.concatenate([own_more[:, :1024], other_more[...]], axis=0)
    total = jnp.dot(rows, weight[:1024, :], preferred_element_type=F32)
    total += jnp.dot(rows_more, weight[1024:, :], preferred_element_type=F32)
    v_own[...] = total[:128]
    v_other[...] = total[128:]
    grads = jnp.concatenate([own[:, 1024:], other[:, 1024:]], axis=0)
    for part in range(4):
        cols = slice(part * 512, (part + 1) * 512)
        piece = lax.dot_general(
            grads, weight[cols, :], (((1,), (1,)), ((), ())), preferred_element_type=F32
        ).astype(BF16)
        g_own[:, cols] = piece[:128]
        g_other[:, cols] = piece[128:]


def finish_kernel(place, v_own, v_other, g_own, g_other, values, input_grad):
    values[...] = (v_own[...] + v_other[...]).astype(BF16)
    for p in range(4):
        grad = (g_own, g_other)[p % 2]
        wanted = jnp.bitwise_xor(place[0], p)
        for m in range(8):
            at = (p // 2) * 1024 + m * 128
            input_grad[:, lanes(4 * m + wanted)] = grad[:, at : at + 128]


def outer_kernel(chosen, outer, momentum, summed, new_outer, new_momentum):
    k = chosen[0]
    new_outer[...] = outer[...]
    new_momentum[...] = momentum[...]
    pseudo = summed[...] * (1.0 / 16)
    moment = 0.9 * momentum[k] + pseudo
    new_momentum[k] = moment
    new_outer[k] = outer[k] - 0.7 * (pseudo + 0.9 * moment)


def partner(core, z):
    return z ^ 1 if core == 0 else ((z + 1) % 16 if z % 2 else (z - 1) % 16)


def swaps():
    z_pairs, diagonal = [], []
    for core in range(2):
        for z in range(16):
            here, there = core * 16 + z, core * 16 + partner(core, z)
            z_pairs.append((here, there))
            diagonal += [(2 * here + y, 2 * there + 1 - y) for y in range(2)]
    return (
        lambda a: a,
        lambda a: lax.ppermute(a, "yhi", [(0, 1), (1, 0)]),
        lambda a: lax.ppermute(a, ("core", "z"), z_pairs),
        lambda a: lax.ppermute(a, ("core", "z", "yhi"), diagonal),
    )


def body(tokens, v_weight, out_grad, outer_params, momentum, snapshot, frag_index):
    z, y = lax.axis_index("z"), lax.axis_index("yhi")
    place = jnp.stack([2 * lax.rem(z, 2) + y, lax.div(z, 2)]).astype(jnp.int32)
    swap = swaps()
    gathered = lax.all_gather(v_weight[0], "z", axis=0, tiled=True)

    packed = local(pack_kernel, [((128, 1536), BF16)] * 4 + [((128, 1024), BF16)], "pack", (place, tokens, out_grad))
    packs = [swap[p](packed[p]) for p in range(4)]
    (partial,) = local(weight_grad_kernel, [((1024, 512), F32)], "weight_grad", (place, *packs))
    rings = [[z_of for z_of in range(16) if z_of % 2 == odd] for odd in range(2)]
    summed = lax.psum_scatter(partial, "z", scatter_dimension=0, axis_index_groups=rings, tiled=True)
    weight_grad = (summed * (1.0 / math.sqrt(4096))).astype(BF16)[None]

    more, chosen = lax.optimization_barrier((packed[4], frag_index, partial))[:2]
    more = swap[1](more)
    outer_now = lax.dynamic_index_in_dim(outer_params, chosen[0], 0, keepdims=False)
    snap = lax.dynamic_index_in_dim(snapshot[0], chosen[0], 0, keepdims=False)
    exchange = functools.partial(lax.all_to_all, axis_name=REPLICA, split_axis=0, concat_axis=0, tiled=True)
    diff = exchange(outer_now - snap.astype(F32)).reshape(16, 8, 512).sum(0)
    diff = exchange(jnp.tile(diff, (16, 1)))
    new_outer, new_momentum = local(
        outer_kernel, [((4, 128, 512), F32)] * 2, "outer", (chosen, outer_params, momentum, diff)
    )

    place = lax.optimization_barrier((place, new_momentum))[0]
    v_own, v_other, g_own, g_other = pl.pallas_call(
        project_kernel,
        out_shape=[jax.ShapeDtypeStruct((128, 512), F32)] * 2 + [jax.ShapeDtypeStruct((128, 2048), BF16)] * 2,
        in_specs=[SMEM] + [VMEM] * 5,
        out_specs=[VMEM] * 4,
        scratch_shapes=[pltpu.VMEM((2048, 512), BF16)],
        name="project",
        compiler_params=pltpu.CompilerParams(vmem_limit_bytes=40 * 2**20),
    )(place, packs[0], packed[2], packs[1], more, gathered)
    v_own = lax.optimization_barrier((v_own, weight_grad))[0]
    values, input_grad = local(
        finish_kernel,
        [((128, 512), BF16), ((128, 4096), BF16)],
        "finish",
        (place, v_own, swap[1](v_other), g_own, swap[1](g_other)),
    )
    return (values, input_grad, weight_grad, new_outer, new_momentum)


def solution(mesh):
    fine = Mesh(mesh.devices.reshape(2, 4, 2, 16, 2), EVERY)
    fsdp = ("z", "yhi")
    in_specs = (
        P(EVERY, None),
        P(REPLICA, fsdp, None),
        P(EVERY, None),
        P(None, fsdp, None),
        P(None, fsdp, None),
        P(REPLICA, None, fsdp, None),
        P(),
    )
    out_specs = (
        P(EVERY, None),
        P(EVERY, None),
        P(REPLICA, fsdp, None),
        P(None, fsdp, None),
        P(None, fsdp, None),
    )
    return jax.shard_map(body, mesh=fine, in_specs=in_specs, out_specs=out_specs, check_vma=False)
```

```python
import functools
import math

import jax
import jax.numpy as jnp
from jax import lax
from jax.experimental import pallas as pl
from jax.experimental.pallas import tpu as pltpu
from jax.sharding import Mesh
from jax.sharding import PartitionSpec as P

REPLICA = ("ylo", "x", "core")
EVERY = REPLICA + ("z", "yhi")
F32, BF16 = jnp.float32, jnp.bfloat16
VMEM = pl.BlockSpec(memory_space=pltpu.VMEM)
SMEM = pl.BlockSpec(memory_space=pltpu.SMEM)


def local(kernel, outs, name, ins, scratch=()):
    return pl.pallas_call(
        kernel,
        out_shape=[jax.ShapeDtypeStruct(s, d) for s, d in outs],
        in_specs=[SMEM] + [VMEM] * (len(ins) - 1),
        out_specs=[VMEM] * len(outs),
        scratch_shapes=scratch,
        name=name,
        compiler_params=pltpu.CompilerParams(vmem_limit_bytes=40 * 2**20),
    )(*ins)


def lanes(block, width=128):
    return pl.ds(pl.multiple_of(block * width, width), width)


def pack_kernel(place, tokens, out_grad, *packs):
    for p, pack in enumerate(packs):
        wanted = jnp.bitwise_xor(place[0], min(p, 3))
        for m in range(8):
            pack[:, m * 128 : (m + 1) * 128] = tokens[:, lanes(4 * m + wanted)]
        if p < 4:
            pack[:, 1024:] = out_grad[...]


def weight_grad_kernel(place, p0, p1, p2, p3, out):
    both = jnp.concatenate([p[...] for p in (p0, p1, p2, p3)], axis=0)
    grads = both[:, 1024:]
    for part in range(4):
        cols = slice(part * 256, (part + 1) * 256)
        out[cols, :] = lax.dot_general(
            both[:, cols], grads, (((0,), (0,)), ((), ())), preferred_element_type=F32
        )


def by_class(place, gathered, weight):
    parity = lax.shift_right_logical(place[0], 1)
    for half in range(2):
        for m in range(8):
            row = pl.multiple_of((2 * m + jnp.bitwise_xor(parity, half)) * 128, 128)
            weight[half * 1024 + m * 128 : half * 1024 + (m + 1) * 128, :] = gathered[pl.ds(row, 128), :]


def input_grad_kernel(place, own, other, gathered, g_own, g_other, weight):
    by_class(place, gathered, weight)
    grads = jnp.concatenate([own[:, 1024:], other[:, 1024:]], axis=0)
    for part in range(4):
        cols = slice(part * 512, (part + 1) * 512)
        piece = lax.dot_general(
            grads, weight[cols, :], (((1,), (1,)), ((), ())), preferred_element_type=F32
        ).astype(BF16)
        g_own[:, cols] = piece[:128]
        g_other[:, cols] = piece[128:]


def values_kernel(place, own, own_more, other, other_more, gathered, v_own, v_other, weight):
    by_class(place, gathered, weight)
    rows = jnp.concatenate([own[:, :1024], other[:, :1024]], axis=0)
    rows_more = jnp.concatenate([own_more[:, :1024], other_more[...]], axis=0)
    total = jnp.dot(rows, weight[:1024, :], preferred_element_type=F32)
    total += jnp.dot(rows_more, weight[1024:, :], preferred_element_type=F32)
    v_own[...] = total[:128]
    v_other[...] = total[128:]


def finish_kernel(place, v_own, v_other, g_own, g_other, values, input_grad):
    values[...] = (v_own[...] + v_other[...]).astype(BF16)
    for p in range(4):
        grad = (g_own, g_other)[p % 2]
        wanted = jnp.bitwise_xor(place[0], p)
        for m in range(8):
            at = (p // 2) * 1024 + m * 128
            input_grad[:, lanes(4 * m + wanted)] = grad[:, at : at + 128]


def outer_kernel(chosen, outer, momentum, summed, new_outer, new_momentum):
    k = chosen[0]
    new_outer[...] = outer[...]
    new_momentum[...] = momentum[...]
    pseudo = summed[...] * (1.0 / 16)
    moment = 0.9 * momentum[k] + pseudo
    new_momentum[k] = moment
    new_outer[k] = outer[k] - 0.7 * (pseudo + 0.9 * moment)


def partner(core, z):
    return z ^ 1 if core == 0 else ((z + 1) % 16 if z % 2 else (z - 1) % 16)


def swaps():
    z_pairs, diagonal = [], []
    for core in range(2):
        for z in range(16):
            here, there = core * 16 + z, core * 16 + partner(core, z)
            z_pairs.append((here, there))
            diagonal += [(2 * here + y, 2 * there + 1 - y) for y in range(2)]
    return (
        lambda a: a,
        lambda a: lax.ppermute(a, "yhi", [(0, 1), (1, 0)]),
        lambda a: lax.ppermute(a, ("core", "z"), z_pairs),
        lambda a: lax.ppermute(a, ("core", "z", "yhi"), diagonal),
    )


def body(tokens, v_weight, out_grad, outer_params, momentum, snapshot, frag_index):
    z, y = lax.axis_index("z"), lax.axis_index("yhi")
    place = jnp.stack([2 * lax.rem(z, 2) + y, lax.div(z, 2)]).astype(jnp.int32)
    swap = swaps()
    gathered = lax.all_gather(v_weight[0], "z", axis=0, tiled=True)

    packed = local(pack_kernel, [((128, 1536), BF16)] * 4 + [((128, 1024), BF16)], "pack", (place, tokens, out_grad))
    packs = [swap[p](packed[p]) for p in range(4)]
    exchange = functools.partial(lax.all_to_all, axis_name=REPLICA, split_axis=0, concat_axis=0, tiled=True)
    outer_now = lax.dynamic_index_in_dim(outer_params, frag_index[0], 0, keepdims=False)
    snap = lax.dynamic_index_in_dim(snapshot[0], frag_index[0], 0, keepdims=False)
    ready, *_ = lax.optimization_barrier((outer_now - snap.astype(F32), packed[0]))
    diffs = exchange(ready)

    mine = lax.optimization_barrier((packs[0], diffs))[0]
    (partial,) = local(weight_grad_kernel, [((1024, 512), F32)], "weight_grad", (place, mine, *packs[1:]))
    rings = [[z_of for z_of in range(16) if z_of % 2 == odd] for odd in range(2)]
    summed = lax.psum_scatter(partial, "z", scatter_dimension=0, axis_index_groups=rings, tiled=True)
    weight_grad = (summed * (1.0 / math.sqrt(4096))).astype(BF16)[None]

    more, diffs = lax.optimization_barrier((packed[4], diffs, partial))[:2]
    more = swap[1](more)
    diff = exchange(jnp.tile(diffs.reshape(16, 8, 512).sum(0), (16, 1)))
    new_outer, new_momentum = local(
        outer_kernel, [((4, 128, 512), F32)] * 2, "outer", (frag_index, outer_params, momentum, diff)
    )

    place = lax.optimization_barrier((place, new_momentum))[0]
    scratch = [pltpu.VMEM((2048, 512), BF16)]
    g_own, g_other = local(
        input_grad_kernel, [((128, 2048), BF16)] * 2, "input_grad", (place, packs[0], packs[1], gathered), scratch
    )
    v_own, v_other = local(
        values_kernel,
        [((128, 512), F32)] * 2,
        "project",
        (place, packs[0], packed[2], packs[1], more, gathered),
        scratch,
    )
    v_own = lax.optimization_barrier((v_own, weight_grad))[0]
    values, input_grad = local(
        finish_kernel,
        [((128, 512), BF16), ((128, 4096), BF16)],
        "finish",
        (place, v_own, swap[1](v_other), g_own, swap[1](g_other)),
    )
    return (values, input_grad, weight_grad, new_outer, new_momentum)


def solution(mesh):
    fine = Mesh(mesh.devices.reshape(2, 4, 2, 16, 2), EVERY)
    fsdp = ("z", "yhi")
    in_specs = (
        P(EVERY, None),
        P(REPLICA, fsdp, None),
        P(EVERY, None),
        P(None, fsdp, None),
        P(None, fsdp, None),
        P(REPLICA, None, fsdp, None),
        P(),
    )
    out_specs = (
        P(EVERY, None),
        P(EVERY, None),
        P(REPLICA, fsdp, None),
        P(None, fsdp, None),
        P(None, fsdp, None),
    )
    return jax.shard_map(body, mesh=fine, in_specs=in_specs, out_specs=out_specs, check_vma=False)
```

```python
import functools
import math

import jax
import jax.numpy as jnp
from jax import lax
from jax.experimental import pallas as pl
from jax.experimental.pallas import tpu as pltpu
from jax.sharding import Mesh
from jax.sharding import PartitionSpec as P

REPLICA = ("ylo", "x", "core")
EVERY = REPLICA + ("z", "yhi")
F32, BF16 = jnp.float32, jnp.bfloat16
VMEM = pl.BlockSpec(memory_space=pltpu.VMEM)
SMEM = pl.BlockSpec(memory_space=pltpu.SMEM)


def local(kernel, outs, name, ins, scratch=()):
    return pl.pallas_call(
        kernel,
        out_shape=[jax.ShapeDtypeStruct(s, d) for s, d in outs],
        in_specs=[SMEM] + [VMEM] * (len(ins) - 1),
        out_specs=[VMEM] * len(outs),
        scratch_shapes=scratch,
        name=name,
        compiler_params=pltpu.CompilerParams(vmem_limit_bytes=40 * 2**20),
    )(*ins)


def lanes(block, width=128):
    return pl.ds(pl.multiple_of(block * width, width), width)


def pack_kernel(place, tokens, out_grad, *packs):
    for p, pack in enumerate(packs):
        wanted = jnp.bitwise_xor(place[0], min(p, 3))
        for m in range(8):
            pack[:, m * 128 : (m + 1) * 128] = tokens[:, lanes(4 * m + wanted)]
        if p < 4:
            pack[:, 1024:] = out_grad[...]


def weight_grad_kernel(place, p0, p1, p2, p3, out):
    both = jnp.concatenate([p[...] for p in (p0, p1, p2, p3)], axis=0)
    grads = both[:, 1024:]
    for part in range(4):
        cols = slice(part * 256, (part + 1) * 256)
        out[cols, :] = lax.dot_general(
            both[:, cols], grads, (((0,), (0,)), ((), ())), preferred_element_type=F32
        )


def by_class(place, gathered, weight):
    parity = lax.shift_right_logical(place[0], 1)
    for half in range(2):
        for m in range(8):
            row = pl.multiple_of((2 * m + jnp.bitwise_xor(parity, half)) * 128, 128)
            weight[half * 1024 + m * 128 : half * 1024 + (m + 1) * 128, :] = gathered[pl.ds(row, 128), :]


def input_grad_kernel(place, own, other, gathered, g_own, g_other, weight):
    by_class(place, gathered, weight)
    grads = jnp.concatenate([own[:, 1024:], other[:, 1024:]], axis=0)
    for part in range(4):
        cols = slice(part * 512, (part + 1) * 512)
        piece = lax.dot_general(
            grads, weight[cols, :], (((1,), (1,)), ((), ())), preferred_element_type=F32
        ).astype(BF16)
        g_own[:, cols] = piece[:128]
        g_other[:, cols] = piece[128:]


def values_kernel(place, own, own_more, other, other_more, gathered, v_own, v_other, weight):
    by_class(place, gathered, weight)
    rows = jnp.concatenate([own[:, :1024], other[:, :1024]], axis=0)
    rows_more = jnp.concatenate([own_more[:, :1024], other_more[...]], axis=0)
    total = jnp.dot(rows, weight[:1024, :], preferred_element_type=F32)
    total += jnp.dot(rows_more, weight[1024:, :], preferred_element_type=F32)
    v_own[...] = total[:128]
    v_other[...] = total[128:]


def finish_kernel(place, v_own, v_other, g_own, g_other, values, input_grad):
    values[...] = (v_own[...] + v_other[...]).astype(BF16)
    for p in range(4):
        grad = (g_own, g_other)[p % 2]
        wanted = jnp.bitwise_xor(place[0], p)
        for m in range(8):
            at = (p // 2) * 1024 + m * 128
            input_grad[:, lanes(4 * m + wanted)] = grad[:, at : at + 128]


def outer_kernel(chosen, outer, momentum, summed, new_outer, new_momentum):
    k = chosen[0]
    new_outer[...] = outer[...]
    new_momentum[...] = momentum[...]
    pseudo = summed[...] * (1.0 / 16)
    moment = 0.9 * momentum[k] + pseudo
    new_momentum[k] = moment
    new_outer[k] = outer[k] - 0.7 * (pseudo + 0.9 * moment)


def partner(core, z):
    return z ^ 1 if core == 0 else ((z + 1) % 16 if z % 2 else (z - 1) % 16)


def swaps():
    z_pairs, diagonal = [], []
    for core in range(2):
        for z in range(16):
            here, there = core * 16 + z, core * 16 + partner(core, z)
            z_pairs.append((here, there))
            diagonal += [(2 * here + y, 2 * there + 1 - y) for y in range(2)]
    return (
        lambda a: a,
        lambda a: lax.ppermute(a, "yhi", [(0, 1), (1, 0)]),
        lambda a: lax.ppermute(a, ("core", "z"), z_pairs),
        lambda a: lax.ppermute(a, ("core", "z", "yhi"), diagonal),
    )


def body(tokens, v_weight, out_grad, outer_params, momentum, snapshot, frag_index):
    z, y = lax.axis_index("z"), lax.axis_index("yhi")
    place = jnp.stack([2 * lax.rem(z, 2) + y, lax.div(z, 2)]).astype(jnp.int32)
    swap = swaps()
    gathered = lax.all_gather(v_weight[0], "z", axis=0, tiled=True)

    packed = local(pack_kernel, [((128, 1536), BF16)] * 4 + [((128, 1024), BF16)], "pack", (place, tokens, out_grad))
    packs = [swap[p](packed[p]) for p in range(4)]
    exchange = functools.partial(lax.all_to_all, axis_name=REPLICA, split_axis=0, concat_axis=0, tiled=True)
    outer_now = lax.dynamic_index_in_dim(outer_params, frag_index[0], 0, keepdims=False)
    snap = lax.dynamic_index_in_dim(snapshot[0], frag_index[0], 0, keepdims=False)
    ready, *_ = lax.optimization_barrier((outer_now - snap.astype(F32), packed[0]))
    diffs = exchange(ready)

    more = swap[1](packed[4])
    mine = lax.optimization_barrier((packs[0], diffs, more))[0]
    (partial,) = local(weight_grad_kernel, [((1024, 512), F32)], "weight_grad", (place, mine, *packs[1:]))
    rings = [[z_of for z_of in range(16) if z_of % 2 == odd] for odd in range(2)]
    summed = lax.psum_scatter(partial, "z", scatter_dimension=0, axis_index_groups=rings, tiled=True)
    weight_grad = (summed * (1.0 / math.sqrt(4096))).astype(BF16)[None]

    diffs = lax.optimization_barrier((diffs, partial))[0]
    diff = exchange(jnp.tile(diffs.reshape(16, 8, 512).sum(0), (16, 1)))
    new_outer, new_momentum = local(
        outer_kernel, [((4, 128, 512), F32)] * 2, "outer", (frag_index, outer_params, momentum, diff)
    )

    place = lax.optimization_barrier((place, new_momentum))[0]
    scratch = [pltpu.VMEM((2048, 512), BF16)]
    g_own, g_other = local(
        input_grad_kernel, [((128, 2048), BF16)] * 2, "input_grad", (place, packs[0], packs[1], gathered), scratch
    )
    v_own, v_other = local(
        values_kernel,
        [((128, 512), F32)] * 2,
        "project",
        (place, packs[0], packed[2], packs[1], more, gathered),
        scratch,
    )
    v_own = lax.optimization_barrier((v_own, weight_grad))[0]
    values, input_grad = local(
        finish_kernel,
        [((128, 512), BF16), ((128, 4096), BF16)],
        "finish",
        (place, v_own, swap[1](v_other), g_own, swap[1](g_other)),
    )
    return (values, input_grad, weight_grad, new_outer, new_momentum)


def solution(mesh):
    fine = Mesh(mesh.devices.reshape(2, 4, 2, 16, 2), EVERY)
    fsdp = ("z", "yhi")
    in_specs = (
        P(EVERY, None),
        P(REPLICA, fsdp, None),
        P(EVERY, None),
        P(None, fsdp, None),
        P(None, fsdp, None),
        P(REPLICA, None, fsdp, None),
        P(),
    )
    out_specs = (
        P(EVERY, None),
        P(EVERY, None),
        P(REPLICA, fsdp, None),
        P(None, fsdp, None),
        P(None, fsdp, None),
    )
    return jax.shard_map(body, mesh=fine, in_specs=in_specs, out_specs=out_specs, check_vma=False)
```

```python
import functools
import math

import jax
import jax.numpy as jnp
from jax import lax
from jax.experimental import pallas as pl
from jax.experimental.pallas import tpu as pltpu
from jax.sharding import Mesh
from jax.sharding import PartitionSpec as P

REPLICA = ("ylo", "x", "core")
EVERY = REPLICA + ("z", "yhi")
F32, BF16 = jnp.float32, jnp.bfloat16
VMEM = pl.BlockSpec(memory_space=pltpu.VMEM)
SMEM = pl.BlockSpec(memory_space=pltpu.SMEM)


def local(kernel, outs, name, ins, scratch=()):
    return pl.pallas_call(
        kernel,
        out_shape=[jax.ShapeDtypeStruct(s, d) for s, d in outs],
        in_specs=[SMEM] + [VMEM] * (len(ins) - 1),
        out_specs=[VMEM] * len(outs),
        scratch_shapes=scratch,
        name=name,
        compiler_params=pltpu.CompilerParams(vmem_limit_bytes=40 * 2**20),
    )(*ins)


def lanes(block, width=128):
    return pl.ds(pl.multiple_of(block * width, width), width)


def pack_kernel(place, tokens, out_grad, *packs):
    for p, pack in enumerate(packs):
        wanted = jnp.bitwise_xor(place[0], min(p, 3))
        for m in range(8):
            pack[:, m * 128 : (m + 1) * 128] = tokens[:, lanes(4 * m + wanted)]
        if p < 4:
            pack[:, 1024:] = out_grad[...]


def weight_grad_kernel(place, p0, p1, p2, p3, out):
    both = jnp.concatenate([p[...] for p in (p0, p1, p2, p3)], axis=0)
    grads = both[:, 1024:]
    for part in range(4):
        cols = slice(part * 256, (part + 1) * 256)
        out[cols, :] = lax.dot_general(
            both[:, cols], grads, (((0,), (0,)), ((), ())), preferred_element_type=F32
        )


def by_class(place, gathered, weight):
    parity = lax.shift_right_logical(place[0], 1)
    for half in range(2):
        for m in range(8):
            row = pl.multiple_of((2 * m + jnp.bitwise_xor(parity, half)) * 128, 128)
            weight[half * 1024 + m * 128 : half * 1024 + (m + 1) * 128, :] = gathered[pl.ds(row, 128), :]


def input_grad_kernel(place, own, other, gathered, g_own, g_other, weight):
    by_class(place, gathered, weight)
    grads = jnp.concatenate([own[:, 1024:], other[:, 1024:]], axis=0)
    for part in range(4):
        cols = slice(part * 512, (part + 1) * 512)
        piece = lax.dot_general(
            grads, weight[cols, :], (((1,), (1,)), ((), ())), preferred_element_type=F32
        ).astype(BF16)
        g_own[:, cols] = piece[:128]
        g_other[:, cols] = piece[128:]


def values_kernel(place, own, own_more, other, other_more, gathered, v_own, v_other, weight):
    by_class(place, gathered, weight)
    rows = jnp.concatenate([own[:, :1024], other[:, :1024]], axis=0)
    rows_more = jnp.concatenate([own_more[:, :1024], other_more[...]], axis=0)
    total = jnp.dot(rows, weight[:1024, :], preferred_element_type=F32)
    total += jnp.dot(rows_more, weight[1024:, :], preferred_element_type=F32)
    v_own[...] = total[:128]
    v_other[...] = total[128:]


def finish_kernel(place, v_own, v_other, g_own, g_other, values, input_grad):
    values[...] = (v_own[...] + v_other[...]).astype(BF16)
    for p in range(4):
        grad = (g_own, g_other)[p % 2]
        wanted = jnp.bitwise_xor(place[0], p)
        for m in range(8):
            at = (p // 2) * 1024 + m * 128
            input_grad[:, lanes(4 * m + wanted)] = grad[:, at : at + 128]


def outer_kernel(chosen, outer, momentum, summed, new_outer, new_momentum):
    k = chosen[0]
    new_outer[...] = outer[...]
    new_momentum[...] = momentum[...]
    pseudo = summed[...] * (1.0 / 16)
    moment = 0.9 * momentum[k] + pseudo
    new_momentum[k] = moment
    new_outer[k] = outer[k] - 0.7 * (pseudo + 0.9 * moment)


def partner(core, z):
    return z ^ 1 if core == 0 else ((z + 1) % 16 if z % 2 else (z - 1) % 16)


def swaps():
    z_pairs, diagonal = [], []
    for core in range(2):
        for z in range(16):
            here, there = core * 16 + z, core * 16 + partner(core, z)
            z_pairs.append((here, there))
            diagonal += [(2 * here + y, 2 * there + 1 - y) for y in range(2)]
    return (
        lambda a: a,
        lambda a: lax.ppermute(a, "yhi", [(0, 1), (1, 0)]),
        lambda a: lax.ppermute(a, ("core", "z"), z_pairs),
        lambda a: lax.ppermute(a, ("core", "z", "yhi"), diagonal),
    )


def body(tokens, v_weight, out_grad, outer_params, momentum, snapshot, frag_index):
    z, y = lax.axis_index("z"), lax.axis_index("yhi")
    place = jnp.stack([2 * lax.rem(z, 2) + y, lax.div(z, 2)]).astype(jnp.int32)
    swap = swaps()
    gathered = lax.all_gather(v_weight[0], "z", axis=0, tiled=True)

    packed = local(pack_kernel, [((128, 1536), BF16)] * 4 + [((128, 1024), BF16)], "pack", (place, tokens, out_grad))
    packs = [swap[p](packed[p]) for p in range(4)]
    exchange = functools.partial(lax.all_to_all, axis_name=REPLICA, split_axis=0, concat_axis=0, tiled=True)
    outer_now = lax.dynamic_index_in_dim(outer_params, frag_index[0], 0, keepdims=False)
    snap = lax.dynamic_index_in_dim(snapshot[0], frag_index[0], 0, keepdims=False)
    ready, *_ = lax.optimization_barrier((outer_now - snap.astype(F32), packed[0]))
    diffs = jnp.tile(exchange(ready).reshape(16, 8, 512).sum(0), (16, 1))

    more = swap[1](packed[4])
    mine = lax.optimization_barrier((packs[0], diffs, more))[0]
    (partial,) = local(weight_grad_kernel, [((1024, 512), F32)], "weight_grad", (place, mine, *packs[1:]))
    rings = [[z_of for z_of in range(16) if z_of % 2 == odd] for odd in range(2)]
    summed = lax.psum_scatter(partial, "z", scatter_dimension=0, axis_index_groups=rings, tiled=True)
    weight_grad = (summed * (1.0 / math.sqrt(4096))).astype(BF16)[None]

    diffs = lax.optimization_barrier((diffs, partial))[0]
    diff = exchange(diffs)
    new_outer, new_momentum = local(
        outer_kernel, [((4, 128, 512), F32)] * 2, "outer", (frag_index, outer_params, momentum, diff)
    )

    place = lax.optimization_barrier((place, new_momentum))[0]
    scratch = [pltpu.VMEM((2048, 512), BF16)]
    g_own, g_other = local(
        input_grad_kernel, [((128, 2048), BF16)] * 2, "input_grad", (place, packs[0], packs[1], gathered), scratch
    )
    v_own, v_other = local(
        values_kernel,
        [((128, 512), F32)] * 2,
        "project",
        (place, packs[0], packed[2], packs[1], more, gathered),
        scratch,
    )
    v_own = lax.optimization_barrier((v_own, weight_grad))[0]
    values, input_grad = local(
        finish_kernel,
        [((128, 512), BF16), ((128, 4096), BF16)],
        "finish",
        (place, v_own, swap[1](v_other), g_own, swap[1](g_other)),
    )
    return (values, input_grad, weight_grad, new_outer, new_momentum)


def solution(mesh):
    fine = Mesh(mesh.devices.reshape(2, 4, 2, 16, 2), EVERY)
    fsdp = ("z", "yhi")
    in_specs = (
        P(EVERY, None),
        P(REPLICA, fsdp, None),
        P(EVERY, None),
        P(None, fsdp, None),
        P(None, fsdp, None),
        P(REPLICA, None, fsdp, None),
        P(),
    )
    out_specs = (
        P(EVERY, None),
        P(EVERY, None),
        P(REPLICA, fsdp, None),
        P(None, fsdp, None),
        P(None, fsdp, None),
    )
    return jax.shard_map(body, mesh=fine, in_specs=in_specs, out_specs=out_specs, check_vma=False)
```
